256 devices in a mesh: dp: 8 (over x, y_hi), expert: 32 (over z, y_lo, core).
Axes of the slice: x: 4, y: 4 (y_hi: 2, y_lo: 2; y = y_hi * 2 + y_lo), z: 8, core: 2. Of those that a mesh axis runs over, the one named last changes fastest.
Arguments:
- tokens: bfloat16 [3072, 4096], P(('dp', 'expert')), may hold values from -6 to 6
- expert_ids: int32 [3072, 8], P(('dp', 'expert')), may hold values from 0 to 63, all different within a row; in each aligned block of 12 rows (0 to 11, 12 to 23, ...) at most 3 rows name the same one
- gate_probs: float32 [3072, 8], P(('dp', 'expert')), may hold values from 0.02 to 5
- in_weight: bfloat16 [64, 4096, 3072], P('expert', None, 'dp'), may hold values from -0.09375 to 0.09375
- out_weight: bfloat16 [64, 1536, 4096], P('expert', 'dp'), may hold values from -0.15625 to 0.15625
- swap_slot: int32 [32], replicated, may hold values from 0 to 1
Outputs:
- mixed_out: bfloat16 [3072, 4096], P(('dp', 'expert'))
- owner_load: float32 [32], replicated
The draws below stay inside these ranges and needn't reach their ends.
Inputs may be any that keep to these rules, and one draw needn't show every extreme that they name: `expert_ids`: among the rows of one device no expert is named more than 3 times, and in every draw some device's rows name some expert exactly 3 times; a row names 8 different experts.
All inputs are finite; a program needn't handle non-finite values.
Results may differ from the reference program's by a relative error of at most 0.018.
Values may be sent and summed in bfloat16 or wider, within the bound.
A program may use at most 128 MiB of HBM per device.

```python
import math
import jax
import jax.numpy as jnp
import numpy as np
from jax import lax

D = 4096
FF = 1536
TOP = 8
EXP_DEV = 2
TOK_DEV = 12
EXPERTS = 64
OWNERS = 32
CAP = 3
TOKENS = 3072
N_DP = 8


def draw_gate_probs(key, part):
    key = jax.random.fold_in(key, 5)
    rows = jnp.arange(TOKENS, dtype=jnp.float32)[:, None] / TOKENS
    logs = jax.random.uniform(key, (TOKENS, TOP), jnp.float32, jnp.log(0.02), jnp.log(0.5))
    base = jnp.exp(logs)
    scale = 1.0 + 4.0 * rows
    return jnp.clip(base * scale, 0.02, 5.0).astype(jnp.float32)


def plant(entries, own_key, low, top_value):
    longest = entries.shape.index(max(entries.shape))
    spots = []
    for shift in (0, 1):
        where = [jax.random.randint(jax.random.fold_in(own_key, axis), (), 0, length) for axis, length in enumerate(entries.shape)]
        where[longest] = (where[longest] + shift) % entries.shape[longest]
        spots.append(tuple(where))
    return entries.at[spots[0]].set(low).at[spots[1]].set(top_value)


def block_scale(own_key, extent, pieces, smallest, high):
    gain, own = 1.0, jax.random.fold_in(own_key, 6)
    for axis_at, parts in pieces:
        draws = jnp.exp(jax.random.uniform(jax.random.fold_in(own, axis_at), (parts,), jnp.float32, smallest / len(pieces), high / len(pieces)))
        gain = gain * jnp.repeat(draws, extent[axis_at] // parts).reshape([-1 if axis == axis_at else 1 for axis in range(len(extent))])
    return gain


def shared_out(own_key, own, number, rows, amount, top, reach, slope):
    ranking = jax.random.permutation(own_key, amount)
    packed, common = shares(amount, rows * top, reach, slope, True), shares(amount, rows * top, reach, slope, False)
    places = jnp.arange(amount)

    def named(lengths, turn):
        used = int((lengths > 0).sum())
        fixed = max(1, used // 4)
        moved = fixed + (places - fixed + turn * (used - fixed)) % max(1, amount - fixed)
        return jnp.zeros((amount,), jnp.int32).at[ranking[jnp.where(places < fixed, places, moved)]].set(jnp.asarray(lengths, jnp.int32))

    lengths = jnp.where(number % 4 == 0, named(packed, number // 4), named(common, number - number // 4 - 1))
    mixed = jax.random.permutation(jax.random.fold_in(own, 3), amount)
    giver, sink = mixed[0:amount // 2 * 2:2], mixed[1:amount // 2 * 2:2]
    room = jnp.minimum(lengths[giver] - 1, reach - lengths[sink]) // 2
    room = jnp.where((giver == ranking[0]) | (sink == ranking[0]) | (lengths[sink] == 0), 0, jnp.maximum(room, 0))
    moved = jax.random.randint(jax.random.fold_in(own, 4), (amount // 2,), 0, 1 << 20) % (room + 1)
    lengths = lengths.at[giver].add(-moved).at[sink].add(moved)
    labels = jnp.searchsorted(jnp.cumsum(lengths), jnp.arange(rows * top), side="right").astype(jnp.int32)
    listing = labels.reshape(top, rows).T
    listing = listing[jax.random.permutation(jax.random.fold_in(own, 1), rows)]
    turn = jax.random.randint(jax.random.fold_in(own, 2), (rows, 1), 0, top)
    return jnp.take_along_axis(listing, (jnp.arange(top)[None, :] + turn) % top, axis=1)


def shares(number_of, total, bound, slope, full):
    portions = [(1 << 20) // math.isqrt(rank ** slope) + 1 for rank in range(1, number_of + 1)]
    largest = bound if full else min(bound, max(-(-total // number_of), total * portions[0] // sum(portions)))
    least = 1 if total - largest >= number_of - 1 else 0
    given, rest = [largest] + [least] * (number_of - 1), total - largest - least * (number_of - 1)
    while rest > 0:
        candidates = [i for i in range(1, number_of) if given[i] < largest] or [i for i in range(1, number_of) if given[i] < bound]
        whole, left = sum([portions[i] for i in candidates]), rest
        for i in candidates:
            more = min(bound - given[i], max(1, left * portions[i] // whole), rest)
            given[i] = given[i] + more
            rest = rest - more
    return np.array(given)


def gaussian(stream_key, shape, scale, reach, pieces=(), held_as=jnp.bfloat16):
    factor_of = block_scale(stream_key, shape, pieces, -0.22, 0.18) if pieces else 1.0
    result = jax.random.normal(stream_key, shape, jnp.float32) * scale * factor_of
    return jnp.minimum(jnp.maximum(result, -reach), reach).astype(held_as)


def setup_inputs(seed: int = 0) -> dict:
    key_of = jax.random.split(jax.random.key(seed), 7)
    tokens = gaussian(key_of[0], (TOKENS, D), 1.0, 6.0, ((0, 256),))
    expert_ids_keys = jax.random.split(jax.random.fold_in(key_of[1], 1), TOKENS // TOK_DEV)
    expert_ids_turns = jax.random.permutation(jax.random.fold_in(key_of[1], 3), TOKENS // TOK_DEV)
    expert_ids = jax.vmap(lambda own, number: shared_out(jax.random.fold_in(key_of[1], 2), own, number, TOK_DEV, EXPERTS, TOP, CAP, 2))(expert_ids_keys, expert_ids_turns).reshape((TOKENS, TOP))
    gate_probs = draw_gate_probs(jax.random.fold_in(key_of[6], 71), 0)
    in_weight = gaussian(key_of[3], (EXPERTS, D, 2 * FF), D ** -0.5, 0.09375, ((0, 32), (2, 8)))
    out_weight = gaussian(key_of[4], (EXPERTS, FF, D), FF ** -0.5, 0.15625, ((0, 32), (1, 8)))
    swap_slot = plant(jax.random.randint(key_of[5], (OWNERS,), 0, EXP_DEV), jax.random.fold_in(key_of[5], 1), 0, EXP_DEV - 1).astype(jnp.int32)
    return dict(tokens=tokens, expert_ids=expert_ids, gate_probs=gate_probs, in_weight=in_weight, out_weight=out_weight, swap_slot=swap_slot)


def reference(tokens, expert_ids, gate_probs, in_weight, out_weight, swap_slot):
    row_block = 64
    half_width = FF // N_DP
    flat_ids = expert_ids.reshape(-1).astype(jnp.int32)
    assignments = flat_ids.shape[0]
    experts_range = jnp.arange(EXPERTS, dtype=jnp.int32)
    matches = flat_ids[:, None] == experts_range[None, :]
    counts = jnp.sum(matches.astype(jnp.int32), 0).astype(jnp.int32)
    mass = jnp.sum(jnp.where(matches, gate_probs.reshape(-1)[:, None].astype(jnp.float32), jnp.float32(0.0)), 0)
    starts = (jnp.cumsum(counts) - counts).astype(jnp.int32)
    sort_order = jnp.argsort(flat_ids, stable=True).astype(jnp.int32)
    token_rows = jnp.concatenate([(sort_order // TOP).astype(jnp.int32), jnp.zeros((row_block,), jnp.int32)]).astype(jnp.int32)

    def per_expert(expert, sorted_out):
        down_rows = out_weight[expert].astype(jnp.float32).reshape(N_DP, half_width, D)
        up_cols = in_weight[expert]

        def one_block(index, current):
            begin = (starts[expert] + index * row_block).astype(jnp.int32)
            picked = lax.dynamic_slice_in_dim(token_rows, begin, row_block)
            inputs_block = jnp.take(tokens, picked, axis=0)
            both_halves = jnp.dot(inputs_block, up_cols, preferred_element_type=jnp.float32).reshape(row_block, N_DP, 2, half_width)
            hidden = (jax.nn.silu(both_halves[:, :, 0]) * both_halves[:, :, 1]).astype(jnp.bfloat16)
            hidden = lax.optimization_barrier(hidden)
            partials = jnp.einsum("rbf,bfd->rbd", hidden.astype(jnp.float32), down_rows).astype(jnp.bfloat16)
            partials = lax.optimization_barrier(partials)
            block_out = jnp.sum(partials.astype(jnp.float32), 1).astype(jnp.bfloat16)
            return lax.dynamic_update_slice_in_dim(current, block_out, begin, 0)

        block_count = ((counts[expert] + row_block - 1) // row_block).astype(jnp.int32)
        return lax.fori_loop(jnp.int32(0), block_count, one_block, sorted_out)

    sorted_out = lax.fori_loop(0, EXPERTS, per_expert, jnp.zeros((assignments + row_block, D), jnp.bfloat16))
    inverse = jnp.argsort(sort_order).astype(jnp.int32)
    expert_out = jnp.take(sorted_out, inverse, axis=0).reshape(TOKENS, TOP, D)
    mixed_out = jnp.sum(gate_probs[..., None] * expert_out.astype(jnp.float32), 1).astype(jnp.bfloat16)

    home = experts_range // EXP_DEV
    within = experts_range % EXP_DEV
    partner = (home + OWNERS // 2) % OWNERS
    moved = within == swap_slot[home]
    holder = jnp.where(moved, partner, home)
    holder_hot = (holder[:, None] == jnp.arange(OWNERS, dtype=jnp.int32)[None, :]).astype(jnp.float32)
    owner_load = jnp.dot(mass, holder_hot, precision=lax.Precision.HIGHEST) * (OWNERS / TOKENS)
    return mixed_out, owner_load
```

```python
import jax
import jax.numpy as jnp
from jax import lax
from jax.sharding import PartitionSpec as P

BOTH = ("dp", "expert")


def planned_load(mass, swap_slot, per_device, owners, tokens_all):
    experts = jnp.arange(mass.shape[0], dtype=jnp.int32)
    home, within = experts // per_device, experts % per_device
    slot = jnp.repeat(swap_slot, per_device)
    holder = jnp.where(within == slot, (home + owners // 2) % owners, home)
    hot = holder[:, None] == jnp.arange(owners, dtype=jnp.int32)
    return jnp.sum(jnp.where(hot, mass[:, None], 0.0), 0) * (owners / tokens_all)


def on_device(tokens, expert_ids, gate_probs, in_weight, out_weight, swap_slot):
    owners = lax.axis_size("expert")
    per_device, width = in_weight.shape[:2]
    half = out_weight.shape[1]
    experts_all = per_device * owners
    experts = jnp.arange(experts_all, dtype=jnp.int32)
    dense = jnp.sum(
        jnp.where(expert_ids[..., None] == experts, gate_probs[..., None], 0.0), 1
    )
    all_tokens = lax.all_gather(tokens, BOTH, axis=0, tiled=True)
    all_dense = lax.all_gather(dense, BOTH, axis=0, tiled=True)
    load = planned_load(
        jnp.sum(all_dense, 0), swap_slot, per_device, owners, all_tokens.shape[0]
    )
    mine = lax.dynamic_slice_in_dim(
        all_dense, lax.axis_index("expert") * per_device, per_device, 1
    )
    parts = []
    for s in range(per_device):
        both = jnp.dot(all_tokens, in_weight[s], preferred_element_type=jnp.float32)
        hidden = jax.nn.silu(both[:, :half]) * both[:, half:] * mine[:, s : s + 1]
        parts.append(hidden.astype(jnp.bfloat16))
    mixed = jnp.dot(
        jnp.concatenate(parts, 1),
        out_weight.reshape(per_device * half, width),
        preferred_element_type=jnp.float32,
    ).astype(jnp.bfloat16)
    out = lax.psum_scatter(mixed, BOTH, scatter_dimension=0, tiled=True)
    return out, load


def solution(mesh):
    return jax.shard_map(
        on_device,
        mesh=mesh,
        in_specs=(
            P(BOTH, None),
            P(BOTH, None),
            P(BOTH, None),
            P("expert", None, "dp"),
            P("expert", "dp", None),
            P(),
        ),
        out_specs=(P(BOTH, None), P()),
        check_vma=False,
    )
```

```python
import jax
import jax.numpy as jnp
from jax import lax
from jax.experimental import pallas as pl
from jax.experimental.pallas import tpu as pltpu
from jax.sharding import PartitionSpec as P

MESH = pl.DeviceIdType.MESH
BOTH = ("dp", "expert")
NX, NYH, NYL, NZ = 4, 2, 2, 8
NY = NYH * NYL
TILE = 16
GATES = 128
BF, F32 = jnp.bfloat16, jnp.float32


def coordinates():
    dp, ex = lax.axis_index("dp"), lax.axis_index("expert")
    x, yh = dp // NYH, dp % NYH
    core, zy = ex % 2, ex // 2
    return x, yh * NYL + zy % NYL, zy // NYL, core


class Part:
    def __init__(self, at, ring, quad, mid, refs, sems):
        self.at, self.ring, self.quad, self.mid = at, ring, quad, mid
        self.n, self.nq, self.m = ring[1], quad[1], mid[1]
        self.r = TILE * self.m
        self.T, self.ACC, self.SP, self.ST, self.S1, self.S4, self.SUM4, self.S5, self.SUM5, self.S6 = refs
        self.sems = sems


def part_scratch(n, nq, m, width):
    r, q = TILE * m, width // nq
    shapes = [
        (2, n, r, width + GATES),
        (n, r, width),
        (2, r, width),
        (nq, TILE, q + GATES),
        (r, q + GATES),
        (nq, r, q),
        (r, q),
        (m, TILE, q),
        (TILE, q),
        (TILE, width),
    ]
    counts = [nq, m, nq, n, n + 1, n + 1, nq, m, nq]
    sems = [pltpu.SemaphoreType.DMA((c,)) for c in counts for _ in range(2)]
    sems += [pltpu.SemaphoreType.DMA((n + 1, 4)) for _ in range(2)]
    sems += [pltpu.SemaphoreType.REGULAR]
    return [pltpu.VMEM(s, BF) for s in shapes], sems


NBUF, NSEM = 10, 21


def kernel(x_ref, w1_hbm, w2_hbm, out_ref, mass_ref, *scratch):
    x, y, z, core = coordinates()
    sib_core = 1 - core
    d = 1 - 2 * core
    ex, dp = lax.axis_index("expert"), lax.axis_index("dp")
    width = out_ref.shape[2]
    half = w1_hbm.shape[2] // 2

    def dev(ax, i):
        if ax == "x":
            return (i * NYH + y // NYL, ex)
        if ax == "y":
            return (x * NYH + i // NYL, (z * NYL + i % NYL) * 2 + core)
        return (dp, (i * NYL + y % NYL) * 2 + core)

    sib = (dp, ex + d)
    axes = {"x": (x, NX, "x"), "y": (y, NY, "y"), "z": (z, NZ, "z")}
    specs = [("z", "y", "x"), ("x", "y", "z"), ("y", "x", "z")]
    parts = []
    for p, (a, b, c) in enumerate(specs):
        refs = scratch[p * NBUF : (p + 1) * NBUF]
        sems = scratch[3 * NBUF + p * NSEM : 3 * NBUF + (p + 1) * NSEM]
        parts.append(Part(p, axes[a], axes[b], axes[c], refs, sems))
    W1, W2, BOTHS, H, WSEM = scratch[3 * (NBUF + NSEM) :]

    loads = []
    for s in range(2):
        loads.append(
            pltpu.make_async_copy(
                w1_hbm.at[s], W1.at[:, pl.ds(s * 2 * half, 2 * half)], WSEM.at[s]
            )
        )
    loads.append(pltpu.make_async_copy(w2_hbm, W2, WSEM.at[2]))
    for load in loads:
        load.start()

    barrier = pltpu.get_barrier_semaphore()
    count = 1
    pl.semaphore_signal(barrier, inc=1, device_id=sib, device_id_type=MESH)
    for ax in "xyz":
        me, n, _ = axes[ax]
        for s in range(1, n):
            pl.semaphore_signal(
                barrier, inc=1, device_id=dev(ax, (me + s) % n), device_id_type=MESH
            )
            count += 1
    pl.semaphore_wait(barrier, count)

    def send(src, dst, ssem, rsem, to):
        pltpu.make_async_remote_copy(
            src_ref=src, dst_ref=dst, send_sem=ssem, recv_sem=rsem, device_id=to, device_id_type=MESH
        ).start()

    def got(dst, sem):
        pltpu.make_async_remote_copy(
            src_ref=dst, dst_ref=dst, send_sem=sem, recv_sem=sem, device_id=sib, device_id_type=MESH
        ).wait_recv()

    def sent(src, sem):
        pltpu.make_async_remote_copy(
            src_ref=src, dst_ref=src, send_sem=sem, recv_sem=sem, device_id=sib, device_id_type=MESH
        ).wait_send()

    def block(i, size):
        return pl.ds(pl.multiple_of(i * size, size), size)

    for p in parts:
        me, n, ax = p.quad
        piece = p.ST.shape[2]
        for s in range(1, n):
            to = (me + s) % n
            send(x_ref.at[p.at, :, block(to, piece)], p.ST.at[me], p.sems[0].at[s], p.sems[1].at[s], dev(ax, to))
    for p in parts:
        me, n, ax = p.quad
        piece = p.ST.shape[2]
        total = x_ref[p.at, :, block(me, piece)].astype(F32)
        for s in range(1, n):
            slot = (me + n - s) % n
            got(p.ST.at[slot], p.sems[1].at[s])
            total = total + p.ST[slot].astype(F32)
        mid, m, max_ = p.mid
        rows = block(mid, TILE)
        p.S1[rows, :] = total.astype(BF)
        for s in range(1, m):
            send(p.S1.at[rows], p.S1.at[rows], p.sems[2].at[s], p.sems[3].at[s], dev(max_, (mid + s) % m))
    for p in parts:
        mid, m, _ = p.mid
        for s in range(1, m):
            got(p.S1.at[block((mid + m - s) % m, TILE)], p.sems[3].at[s])
        me, n, ax = p.quad
        q = width // n
        mine = p.T.at[core, p.ring[0]]
        for s in range(1, n):
            send(p.S1.at[:, pl.ds(0, q)], mine.at[:, block(me, q)], p.sems[4].at[s], p.sems[5].at[s], dev(ax, (me + s) % n))
        p.T[core, p.ring[0], :, block(me, q)] = p.S1[:, :q]
        p.T[core, p.ring[0], :, width:] = p.S1[:, q:]

    def own_chunk(p, t):
        return (p.ring[0] + p.n - d * t) % p.n

    def sib_chunk(p, t):
        return (p.ring[0] + p.n + d * t) % p.n

    def next_dev(p):
        return dev(p.ring[2], (p.ring[0] + p.n + d) % p.n)


    for p in parts:
        me, n, ax = p.quad
        q = width // n
        for s in range(1, n):
            got(p.T.at[core, p.ring[0], :, block((me + n - s) % n, q)], p.sems[5].at[s])
        chunk = p.T.at[core, p.ring[0]]
        send(chunk, chunk, p.sems[6].at[0], p.sems[7].at[0], next_dev(p))
        send(chunk, chunk, p.sems[8].at[p.n], p.sems[9].at[p.n], sib)

    for load in loads:
        load.wait()

    tiles = 4
    tile = width // tiles
    lane = lax.broadcasted_iota(jnp.int32, (1, GATES), 1)
    experts_all = GATES // 2

    def step(p, t):
        n, r = p.n, p.r
        jo, js = own_chunk(p, t), sib_chunk(p, t)

        @pl.when(t < n)
        def _():
            chunk = p.T.at[core, jo]
            got(chunk, p.sems[7].at[t - 1])

            @pl.when(t < n - 1)
            def _():
                send(chunk, chunk, p.sems[6].at[t], p.sems[7].at[t], next_dev(p))

            send(chunk, chunk, p.sems[8].at[t], p.sems[9].at[t], sib)

        got(p.T.at[sib_core, js], p.sems[9].at[t])
        rows = jnp.concatenate([p.T[core, jo, :, :width], p.T[sib_core, js, :, :width]], 0)
        BOTHS[: 2 * r] = jnp.dot(rows, W1[...], preferred_element_type=F32)
        gates = jnp.concatenate([p.T[core, jo, :, width:], p.T[sib_core, js, :, width:]], 0).astype(F32)
        g = []
        for s in range(2):
            e = 2 * ex + s
            pick = (lane == e) | (lane == e + experts_all)
            g.append(jnp.sum(jnp.where(pick, gates, 0.0), 1, keepdims=True))
        first, second = BOTHS[: 2 * r, : 2 * half], BOTHS[: 2 * r, 2 * half :]
        low = lax.broadcasted_iota(jnp.int32, (1, 2 * half), 1) < half
        gate = jnp.where(low, first, pltpu.roll(second, half, 1))
        up = jnp.where(low, pltpu.roll(first, half, 1), second)
        hidden = jax.nn.silu(gate) * up * jnp.where(low, g[0], g[1])
        H[: 2 * r] = hidden.astype(BF)

        def other(j, _):
            cols = block(j, tile)
            p.T[sib_core, js, :, cols] = jnp.dot(
                H[r : 2 * r], W2[:, cols], preferred_element_type=F32
            ).astype(BF)
            return 0

        lax.fori_loop(0, tiles, other, 0)

        slot = t % 2

        @pl.when(t >= 3)
        def _():
            pl.semaphore_wait(p.sems[20], 1)

        send(p.T.at[sib_core, js, :, pl.ds(0, width)], p.SP.at[slot], p.sems[10].at[t], p.sems[11].at[t], sib)
        got(p.SP.at[slot], p.sems[11].at[t])

        def mine(j, _):
            cols = block(j, tile)
            total = jnp.dot(H[:r], W2[:, cols], preferred_element_type=F32) + p.SP[slot, :, cols].astype(F32)
            here = p.ACC.at[t - 1, :, cols]

            @pl.when(t == 1)
            def _():
                here[...] = total.astype(BF)

            @pl.when(t > 1)
            def _():
                got(here, p.sems[19].at[t - 1, j])
                here[...] = (total + here[...].astype(F32)).astype(BF)

            @pl.when(t < n)
            def _():
                send(here, p.ACC.at[t, :, cols], p.sems[18].at[t, j], p.sems[19].at[t, j], next_dev(p))

            return 0

        lax.fori_loop(0, tiles, mine, 0)

        @pl.when(t <= n - 2)
        def _():
            pl.semaphore_signal(p.sems[20], inc=1, device_id=sib, device_id_type=MESH)

    rounds = max(p.n for p in parts)

    def round_(k, _):
        for p in parts:
            every = rounds // p.n
            if every == 1:
                step(p, k)
            else:

                @pl.when(k % every == 0)
                def _(p=p, every=every):
                    step(p, k // every)

        return 0

    lax.fori_loop(1, rounds + 1, round_, 0)

    for p in parts:
        me, n, ax = p.quad
        q = width // n
        for s in range(1, n):
            to = (me + s) % n
            send(p.ACC.at[p.n - 1, :, block(to, q)], p.S4.at[me], p.sems[12].at[s], p.sems[13].at[s], dev(ax, to))
    for p in parts:
        me, n, ax = p.quad
        q = width // n
        total = p.ACC[p.n - 1, :, block(me, q)].astype(F32)
        for s in range(1, n):
            slot = (me + n - s) % n
            got(p.S4.at[slot], p.sems[13].at[s])
            total = total + p.S4[slot].astype(F32)
        p.SUM4[...] = total.astype(BF)
        mid, m, max_ = p.mid
        for s in range(1, m):
            to = (mid + s) % m
            send(p.SUM4.at[block(to, TILE)], p.S5.at[mid], p.sems[14].at[s], p.sems[15].at[s], dev(max_, to))
    for p in parts:
        mid, m, _ = p.mid
        total = p.SUM4[block(mid, TILE), :].astype(F32)
        for s in range(1, m):
            slot = (mid + m - s) % m
            got(p.S5.at[slot], p.sems[15].at[s])
            total = total + p.S5[slot].astype(F32)
        p.SUM5[...] = total.astype(BF)
        me, n, ax = p.quad
        q = width // n
        for s in range(1, n):
            send(p.SUM5, p.S6.at[:, block(me, q)], p.sems[16].at[s], p.sems[17].at[s], dev(ax, (me + s) % n))
        p.S6[:, block(me, q)] = p.SUM5[...]

    mass = jnp.zeros((TILE, GATES), F32)
    for p in parts:

        def add(i, m_, p=p):
            rows = p.T[i // p.n, i % p.n, :, width:].astype(F32)
            for j in range(p.m):
                m_ = m_ + rows[j * TILE : (j + 1) * TILE]
            return m_

        mass = lax.fori_loop(0, 2 * p.n, add, mass)
    mass_ref[...] = mass

    for p in parts:
        me, n, _ = p.quad
        q = width // n
        for s in range(1, n):
            got(p.S6.at[:, block((me + n - s) % n, q)], p.sems[17].at[s])
        out_ref[p.at] = p.S6[...]

    for p in parts:
        q = width // p.nq
        for s in range(1, p.nq):
            sent(p.ST.at[0], p.sems[0].at[s])
            sent(p.S1.at[:, pl.ds(0, q)], p.sems[4].at[s])
            sent(p.S4.at[0], p.sems[12].at[s])
            sent(p.SUM5, p.sems[16].at[s])
        for s in range(1, p.m):
            sent(p.S1.at[pl.ds(0, TILE)], p.sems[2].at[s])
            sent(p.S5.at[0], p.sems[14].at[s])

        def ring_sent(t, _, p=p):
            chunk = p.T.at[core, 0]

            @pl.when(t < p.n)
            def _():
                sent(chunk, p.sems[6].at[t - 1])
                for j in range(tiles):
                    sent(p.ACC.at[0, :, pl.ds(j * tile, tile)], p.sems[18].at[t, j])

            sent(chunk, p.sems[8].at[t])
            sent(p.SP.at[0], p.sems[10].at[t])
            return 0

        lax.fori_loop(1, p.n + 1, ring_sent, 0)


def fused(x, w1, w2, width):
    half = w1.shape[2] // 2
    buffers, sems = [], []
    for n, nq, m in ((NZ, NY, NX), (NX, NY, NZ), (NY, NX, NZ)):
        b, s = part_scratch(n, nq, m, width)
        buffers += b
        sems += s
    most = 2 * TILE * max(NX, NZ)
    return pl.pallas_call(
        kernel,
        out_shape=(
            jax.ShapeDtypeStruct((3, TILE, width), BF),
            jax.ShapeDtypeStruct((TILE, GATES), F32),
        ),
        in_specs=[
            pl.BlockSpec(memory_space=pltpu.VMEM),
            pl.BlockSpec(memory_space=pl.ANY),
            pl.BlockSpec(memory_space=pl.ANY),
        ],
        out_specs=(pl.BlockSpec(memory_space=pltpu.VMEM), pl.BlockSpec(memory_space=pltpu.VMEM)),
        scratch_shapes=[
            *buffers,
            *sems,
            pltpu.VMEM((width, 4 * half), BF),
            pltpu.VMEM((2 * half, width), BF),
            pltpu.VMEM((most, 4 * half), F32),
            pltpu.VMEM((most, 2 * half), BF),
            pltpu.SemaphoreType.DMA((3,)),
        ],
        compiler_params=pltpu.CompilerParams(
            collective_id=0, has_side_effects=True, vmem_limit_bytes=VMEM_LIMIT
        ),
        cost_estimate=pl.CostEstimate(flops=30_000_000_000, bytes_accessed=10_000_000, transcendentals=1_200_000),
    )(x, w1, w2)


VMEM_LIMIT = 63 * 2**20


def planned_load(mass, swap_slot, per_device, owners, tokens_all):
    experts = jnp.arange(mass.shape[0], dtype=jnp.int32)
    home, within = experts // per_device, experts % per_device
    slot = jnp.repeat(swap_slot, per_device)
    holder = jnp.where(within == slot, (home + owners // 2) % owners, home)
    hot = holder[:, None] == jnp.arange(owners, dtype=jnp.int32)
    return jnp.sum(jnp.where(hot, mass[:, None], 0.0), 0) * (owners / tokens_all)


def on_device(tokens, expert_ids, gate_probs, in_weight, out_weight, swap_slot):
    owners, groups = lax.axis_size("expert"), lax.axis_size("dp")
    per_device, width = in_weight.shape[:2]
    half = out_weight.shape[1]
    experts_all = GATES // 2
    experts = jnp.arange(experts_all, dtype=jnp.int32)
    dense = jnp.sum(
        jnp.where(expert_ids[..., None] == experts, gate_probs[..., None], 0.0), 1
    )
    high = lax.reduce_precision(dense, 8, 7)
    gates = jnp.concatenate([high, dense - high], 1).astype(BF)
    x, y, _, _ = coordinates()
    rows = tokens.shape[0] // 3
    blocks = []
    for p, (at, lines) in enumerate(((y, NY), (y, NY), (x, NX))):
        q = width // lines
        mine = slice(p * rows, (p + 1) * rows)
        wide = jnp.concatenate(
            [tokens[mine].reshape(rows, lines, q), jnp.broadcast_to(gates[mine, None], (rows, lines, GATES))], 2
        ).reshape(rows, -1)
        zero = jnp.zeros((TILE, wide.shape[1]), BF)
        blocks.append(lax.dynamic_update_slice_in_dim(zero, wide, at * rows, 0))
    mixed, mass = fused(jnp.stack(blocks), in_weight, out_weight.reshape(per_device * half, width), width)
    out = jnp.concatenate(
        [lax.dynamic_slice_in_dim(mixed[p], at * rows, rows, 0) for p, at in enumerate((y, y, x))], 0
    )
    mass = jnp.sum(mass, 0)
    mass = (mass[:experts_all] + mass[experts_all:])[: per_device * owners]
    load = planned_load(mass, swap_slot, per_device, owners, groups * owners * tokens.shape[0])
    return out, load


def solution(mesh):
    return jax.shard_map(
        on_device,
        mesh=mesh,
        in_specs=(
            P(BOTH, None),
            P(BOTH, None),
            P(BOTH, None),
            P("expert", None, "dp"),
            P("expert", "dp", None),
            P(),
        ),
        out_specs=(P(BOTH, None), P()),
        check_vma=False,
    )
```

```python
import jax
import jax.numpy as jnp
from jax import lax
from jax.experimental import pallas as pl
from jax.experimental.pallas import tpu as pltpu
from jax.sharding import PartitionSpec as P

MESH = pl.DeviceIdType.MESH
BOTH = ("dp", "expert")
NX, NYH, NYL, NZ = 4, 2, 2, 8
NY = NYH * NYL
TILE = 16
GATES = 128
BF, F32 = jnp.bfloat16, jnp.float32


def coordinates():
    dp, ex = lax.axis_index("dp"), lax.axis_index("expert")
    x, yh = dp // NYH, dp % NYH
    core, zy = ex % 2, ex // 2
    return x, yh * NYL + zy % NYL, zy // NYL, core


class Part:
    def __init__(self, at, ring, quad, mid, refs, sems):
        self.at, self.ring, self.quad, self.mid = at, ring, quad, mid
        self.n, self.nq, self.m = ring[1], quad[1], mid[1]
        self.r = TILE * self.m
        self.T, self.ACC, self.SP, self.ST, self.S1, self.S4, self.SUM4, self.S5, self.SUM5, self.S6, self.OWN = refs
        self.sems = sems


def part_scratch(n, nq, m, width):
    r, q = TILE * m, width // nq
    shapes = [
        (2, n, r, width + GATES),
        (n, r, width),
        (2, r, width),
        (nq, TILE, q + GATES),
        (r, q + GATES),
        (nq, r, q),
        (r, q),
        (m, TILE, q),
        (TILE, q),
        (TILE, width),
        (r, width),
    ]
    counts = [nq, m, nq, n, n + 1, n + 1, nq, m, nq]
    sems = [pltpu.SemaphoreType.DMA((c,)) for c in counts for _ in range(2)]
    sems += [pltpu.SemaphoreType.DMA((n + 1, 4)) for _ in range(2)]
    sems += [pltpu.SemaphoreType.REGULAR]
    return [pltpu.VMEM(s, BF) for s in shapes], sems


NBUF, NSEM = 11, 21


def kernel(x_ref, w1_hbm, w2_hbm, out_ref, mass_ref, *scratch):
    x, y, z, core = coordinates()
    sib_core = 1 - core
    d = 1 - 2 * core
    ex, dp = lax.axis_index("expert"), lax.axis_index("dp")
    width = out_ref.shape[2]
    half = w1_hbm.shape[2] // 2

    def dev(ax, i):
        if ax == "x":
            return (i * NYH + y // NYL, ex)
        if ax == "y":
            return (x * NYH + i // NYL, (z * NYL + i % NYL) * 2 + core)
        return (dp, (i * NYL + y % NYL) * 2 + core)

    sib = (dp, ex + d)
    axes = {"x": (x, NX, "x"), "y": (y, NY, "y"), "z": (z, NZ, "z")}
    specs = [("z", "y", "x"), ("x", "y", "z"), ("y", "x", "z")]
    parts = []
    for p, (a, b, c) in enumerate(specs):
        refs = scratch[p * NBUF : (p + 1) * NBUF]
        sems = scratch[3 * NBUF + p * NSEM : 3 * NBUF + (p + 1) * NSEM]
        parts.append(Part(p, axes[a], axes[b], axes[c], refs, sems))
    W1, W2, BOTHS, H, WSEM = scratch[3 * (NBUF + NSEM) :]

    loads = []
    for s in range(2):
        loads.append(
            pltpu.make_async_copy(
                w1_hbm.at[s], W1.at[:, pl.ds(s * 2 * half, 2 * half)], WSEM.at[s]
            )
        )
    loads.append(pltpu.make_async_copy(w2_hbm, W2, WSEM.at[2]))
    for load in loads:
        load.start()

    barrier = pltpu.get_barrier_semaphore()
    count = 1
    pl.semaphore_signal(barrier, inc=1, device_id=sib, device_id_type=MESH)
    for ax in "xyz":
        me, n, _ = axes[ax]
        for s in range(1, n):
            pl.semaphore_signal(
                barrier, inc=1, device_id=dev(ax, (me + s) % n), device_id_type=MESH
            )
            count += 1
    pl.semaphore_wait(barrier, count)

    def send(src, dst, ssem, rsem, to):
        pltpu.make_async_remote_copy(
            src_ref=src, dst_ref=dst, send_sem=ssem, recv_sem=rsem, device_id=to, device_id_type=MESH
        ).start()

    def got(dst, sem):
        pltpu.make_async_remote_copy(
            src_ref=dst, dst_ref=dst, send_sem=sem, recv_sem=sem, device_id=sib, device_id_type=MESH
        ).wait_recv()

    def sent(src, sem):
        pltpu.make_async_remote_copy(
            src_ref=src, dst_ref=src, send_sem=sem, recv_sem=sem, device_id=sib, device_id_type=MESH
        ).wait_send()

    def block(i, size):
        return pl.ds(pl.multiple_of(i * size, size), size)

    def own_chunk(p, t):
        return (p.ring[0] + p.n - d * t) % p.n

    def sib_chunk(p, t):
        return (p.ring[0] + p.n + d * t) % p.n

    def next_dev(p):
        return dev(p.ring[2], (p.ring[0] + p.n + d) % p.n)


    def swap_quarters(p):
        me, n, ax = p.quad
        piece = p.ST.shape[2]
        for s in range(1, n):
            to = (me + s) % n
            send(x_ref.at[p.at, :, block(to, piece)], p.ST.at[me], p.sems[0].at[s], p.sems[1].at[s], dev(ax, to))

    def gather_rows(p):
        me, n, ax = p.quad
        piece = p.ST.shape[2]
        total = x_ref[p.at, :, block(me, piece)].astype(F32)
        for s in range(1, n):
            slot = (me + n - s) % n
            got(p.ST.at[slot], p.sems[1].at[s])
            total = total + p.ST[slot].astype(F32)
        mid, m, max_ = p.mid
        rows = block(mid, TILE)
        p.S1[rows, :] = total.astype(BF)
        for s in range(1, m):
            send(p.S1.at[rows], p.S1.at[rows], p.sems[2].at[s], p.sems[3].at[s], dev(max_, (mid + s) % m))

    def gather_quarters(p):
        mid, m, _ = p.mid
        for s in range(1, m):
            got(p.S1.at[block((mid + m - s) % m, TILE)], p.sems[3].at[s])
        me, n, ax = p.quad
        q = width // n
        mine = p.T.at[core, p.ring[0]]
        for s in range(1, n):
            send(p.S1.at[:, pl.ds(0, q)], mine.at[:, block(me, q)], p.sems[4].at[s], p.sems[5].at[s], dev(ax, (me + s) % n))
        p.T[core, p.ring[0], :, block(me, q)] = p.S1[:, :q]
        p.T[core, p.ring[0], :, width:] = p.S1[:, q:]

    def start_ring(p):
        me, n, ax = p.quad
        q = width // n
        for s in range(1, n):
            got(p.T.at[core, p.ring[0], :, block((me + n - s) % n, q)], p.sems[5].at[s])
        chunk = p.T.at[core, p.ring[0]]
        send(chunk, chunk, p.sems[6].at[0], p.sems[7].at[0], next_dev(p))
        send(chunk, chunk, p.sems[8].at[p.n], p.sems[9].at[p.n], sib)

    A, B, C = parts
    for p in (A, C, B):
        swap_quarters(p)
    for p in (A, C, B):
        gather_rows(p)
    gather_quarters(A)
    start_ring(A)
    gather_quarters(C)
    gather_quarters(B)
    start_ring(C)
    start_ring(B)

    for load in loads:
        load.wait()

    tiles = 4
    tile = width // tiles
    lane = lax.broadcasted_iota(jnp.int32, (1, GATES), 1)
    experts_all = GATES // 2

    def forward(p, t):
        @pl.when(t < p.n)
        def _():
            chunk = p.T.at[core, own_chunk(p, t)]
            got(chunk, p.sems[7].at[t - 1])

            @pl.when(t < p.n - 1)
            def _():
                send(chunk, chunk, p.sems[6].at[t], p.sems[7].at[t], next_dev(p))

            send(chunk, chunk, p.sems[8].at[t], p.sems[9].at[t], sib)

    def compute(p, t):
        r = p.r
        jo, js = own_chunk(p, t), sib_chunk(p, t)
        got(p.T.at[sib_core, js], p.sems[9].at[t])
        rows = jnp.concatenate([p.T[core, jo, :, :width], p.T[sib_core, js, :, :width]], 0)
        BOTHS[: 2 * r] = jnp.dot(rows, W1[...], preferred_element_type=F32)
        gates = jnp.concatenate([p.T[core, jo, :, width:], p.T[sib_core, js, :, width:]], 0).astype(F32)
        g = []
        for s in range(2):
            e = 2 * ex + s
            pick = (lane == e) | (lane == e + experts_all)
            g.append(jnp.sum(jnp.where(pick, gates, 0.0), 1, keepdims=True))
        first, second = BOTHS[: 2 * r, : 2 * half], BOTHS[: 2 * r, 2 * half :]
        low = lax.broadcasted_iota(jnp.int32, (1, 2 * half), 1) < half
        gate = jnp.where(low, first, pltpu.roll(second, half, 1))
        up = jnp.where(low, pltpu.roll(first, half, 1), second)
        hidden = jax.nn.silu(gate) * up * jnp.where(low, g[0], g[1])
        H[: 2 * r] = hidden.astype(BF)

        def down(j, _):
            cols = block(j, tile)
            both = jnp.dot(H[: 2 * r], W2[:, cols], preferred_element_type=F32).astype(BF)
            p.OWN[:, cols] = both[:r]
            p.T[sib_core, js, :, cols] = both[r:]
            return 0

        lax.fori_loop(0, tiles, down, 0)

        @pl.when(t >= 3)
        def _():
            pl.semaphore_wait(p.sems[20], 1)

        send(p.T.at[sib_core, js, :, pl.ds(0, width)], p.SP.at[t % 2], p.sems[10].at[t], p.sems[11].at[t], sib)

    def combine(p, t):
        n, slot = p.n, t % 2
        got(p.SP.at[slot], p.sems[11].at[t])

        def add(j, _):
            cols = block(j, tile)
            here = p.ACC.at[t - 1, :, cols]

            @pl.when(t == 1)
            def _():
                here[...] = (p.OWN[:, cols].astype(F32) + p.SP[slot, :, cols].astype(F32)).astype(BF)

            @pl.when(t > 1)
            def _():
                got(here, p.sems[19].at[t - 1, j])
                total = p.OWN[:, cols].astype(F32) + p.SP[slot, :, cols].astype(F32)
                here[...] = (total + here[...].astype(F32)).astype(BF)

            @pl.when(t < n)
            def _():
                send(here, p.ACC.at[t, :, cols], p.sems[18].at[t, j], p.sems[19].at[t, j], next_dev(p))

            return 0

        lax.fori_loop(0, tiles, add, 0)

        @pl.when(t <= n - 2)
        def _():
            pl.semaphore_signal(p.sems[20], inc=1, device_id=sib, device_id_type=MESH)

    every = A.n // B.n
    assert A.n == every * B.n and B.n == C.n

    def reduce_quarters(p):
        me, n, ax = p.quad
        q = width // n
        for s in range(1, n):
            to = (me + s) % n
            send(p.ACC.at[p.n - 1, :, block(to, q)], p.S4.at[me], p.sems[12].at[s], p.sems[13].at[s], dev(ax, to))

    def reduce_rows(p):
        me, n, ax = p.quad
        q = width // n
        total = p.ACC[p.n - 1, :, block(me, q)].astype(F32)
        for s in range(1, n):
            slot = (me + n - s) % n
            got(p.S4.at[slot], p.sems[13].at[s])
            total = total + p.S4[slot].astype(F32)
        p.SUM4[...] = total.astype(BF)
        mid, m, max_ = p.mid
        for s in range(1, m):
            to = (mid + s) % m
            send(p.SUM4.at[block(to, TILE)], p.S5.at[mid], p.sems[14].at[s], p.sems[15].at[s], dev(max_, to))

    def return_rows(p):
        mid, m, _ = p.mid
        total = p.SUM4[block(mid, TILE), :].astype(F32)
        for s in range(1, m):
            slot = (mid + m - s) % m
            got(p.S5.at[slot], p.sems[15].at[s])
            total = total + p.S5[slot].astype(F32)
        p.SUM5[...] = total.astype(BF)
        me, n, ax = p.quad
        q = width // n
        for s in range(1, n):
            send(p.SUM5, p.S6.at[:, block(me, q)], p.sems[16].at[s], p.sems[17].at[s], dev(ax, (me + s) % n))
        p.S6[:, block(me, q)] = p.SUM5[...]

    def round_(k, _):
        forward(A, every * k - 1)
        compute(A, every * k - 1)
        forward(B, k)
        compute(B, k)
        combine(A, every * k - 1)
        forward(C, k)
        compute(C, k)
        combine(B, k)
        @pl.when(k == B.n)
        def _():
            reduce_quarters(B)

        forward(A, every * k)
        compute(A, every * k)
        combine(C, k)
        @pl.when(k == B.n)
        def _():
            reduce_quarters(C)

        combine(A, every * k)
        @pl.when(k == B.n)
        def _():
            reduce_quarters(A)

        return 0

    lax.fori_loop(1, B.n + 1, round_, 0)

    reduce_rows(B)
    reduce_rows(C)
    reduce_rows(A)
    return_rows(B)
    return_rows(C)
    return_rows(A)

    mass = jnp.zeros((TILE, GATES), F32)
    for p in parts:

        def add(i, m_, p=p):
            rows = p.T[i // p.n, i % p.n, :, width:].astype(F32)
            for j in range(p.m):
                m_ = m_ + rows[j * TILE : (j + 1) * TILE]
            return m_

        mass = lax.fori_loop(0, 2 * p.n, add, mass)
    mass_ref[...] = mass

    for p in parts:
        me, n, _ = p.quad
        q = width // n
        for s in range(1, n):
            got(p.S6.at[:, block((me + n - s) % n, q)], p.sems[17].at[s])
        out_ref[p.at] = p.S6[...]

    for p in parts:
        q = width // p.nq
        for s in range(1, p.nq):
            sent(p.ST.at[0], p.sems[0].at[s])
            sent(p.S1.at[:, pl.ds(0, q)], p.sems[4].at[s])
            sent(p.S4.at[0], p.sems[12].at[s])
            sent(p.SUM5, p.sems[16].at[s])
        for s in range(1, p.m):
            sent(p.S1.at[pl.ds(0, TILE)], p.sems[2].at[s])
            sent(p.S5.at[0], p.sems[14].at[s])

        def ring_sent(t, _, p=p):
            chunk = p.T.at[core, 0]

            @pl.when(t < p.n)
            def _():
                sent(chunk, p.sems[6].at[t - 1])
                for j in range(tiles):
                    sent(p.ACC.at[0, :, pl.ds(j * tile, tile)], p.sems[18].at[t, j])

            sent(chunk, p.sems[8].at[t])
            sent(p.SP.at[0], p.sems[10].at[t])
            return 0

        lax.fori_loop(1, p.n + 1, ring_sent, 0)


def fused(x, w1, w2, width):
    half = w1.shape[2] // 2
    buffers, sems = [], []
    for n, nq, m in ((NZ, NY, NX), (NX, NY, NZ), (NY, NX, NZ)):
        b, s = part_scratch(n, nq, m, width)
        buffers += b
        sems += s
    most = 2 * TILE * max(NX, NZ)
    return pl.pallas_call(
        kernel,
        out_shape=(
            jax.ShapeDtypeStruct((3, TILE, width), BF),
            jax.ShapeDtypeStruct((TILE, GATES), F32),
        ),
        in_specs=[
            pl.BlockSpec(memory_space=pltpu.VMEM),
            pl.BlockSpec(memory_space=pl.ANY),
            pl.BlockSpec(memory_space=pl.ANY),
        ],
        out_specs=(pl.BlockSpec(memory_space=pltpu.VMEM), pl.BlockSpec(memory_space=pltpu.VMEM)),
        scratch_shapes=[
            *buffers,
            *sems,
            pltpu.VMEM((width, 4 * half), BF),
            pltpu.VMEM((2 * half, width), BF),
            pltpu.VMEM((most, 4 * half), F32),
            pltpu.VMEM((most, 2 * half), BF),
            pltpu.SemaphoreType.DMA((3,)),
        ],
        compiler_params=pltpu.CompilerParams(
            collective_id=0, has_side_effects=True, vmem_limit_bytes=VMEM_LIMIT
        ),
        cost_estimate=pl.CostEstimate(flops=30_000_000_000, bytes_accessed=10_000_000, transcendentals=1_200_000),
    )(x, w1, w2)


VMEM_LIMIT = 63 * 2**20


def planned_load(mass, swap_slot, per_device, owners, tokens_all):
    experts = jnp.arange(mass.shape[0], dtype=jnp.int32)
    home, within = experts // per_device, experts % per_device
    slot = jnp.repeat(swap_slot, per_device)
    holder = jnp.where(within == slot, (home + owners // 2) % owners, home)
    hot = holder[:, None] == jnp.arange(owners, dtype=jnp.int32)
    return jnp.sum(jnp.where(hot, mass[:, None], 0.0), 0) * (owners / tokens_all)


def on_device(tokens, expert_ids, gate_probs, in_weight, out_weight, swap_slot):
    owners, groups = lax.axis_size("expert"), lax.axis_size("dp")
    per_device, width = in_weight.shape[:2]
    half = out_weight.shape[1]
    experts_all = GATES // 2
    experts = jnp.arange(experts_all, dtype=jnp.int32)
    dense = jnp.sum(
        jnp.where(expert_ids[..., None] == experts, gate_probs[..., None], 0.0), 1
    )
    high = lax.reduce_precision(dense, 8, 7)
    gates = jnp.concatenate([high, dense - high], 1).astype(BF)
    x, y, _, _ = coordinates()
    rows = tokens.shape[0] // 3
    blocks = []
    for p, (at, lines) in enumerate(((y, NY), (y, NY), (x, NX))):
        q = width // lines
        mine = slice(p * rows, (p + 1) * rows)
        wide = jnp.concatenate(
            [tokens[mine].reshape(rows, lines, q), jnp.broadcast_to(gates[mine, None], (rows, lines, GATES))], 2
        ).reshape(rows, -1)
        zero = jnp.zeros((TILE, wide.shape[1]), BF)
        blocks.append(lax.dynamic_update_slice_in_dim(zero, wide, at * rows, 0))
    mixed, mass = fused(jnp.stack(blocks), in_weight, out_weight.reshape(per_device * half, width), width)
    out = jnp.concatenate(
        [lax.dynamic_slice_in_dim(mixed[p], at * rows, rows, 0) for p, at in enumerate((y, y, x))], 0
    )
    mass = jnp.sum(mass, 0)
    mass = (mass[:experts_all] + mass[experts_all:])[: per_device * owners]
    load = planned_load(mass, swap_slot, per_device, owners, groups * owners * tokens.shape[0])
    return out, load


def solution(mesh):
    return jax.shard_map(
        on_device,
        mesh=mesh,
        in_specs=(
            P(BOTH, None),
            P(BOTH, None),
            P(BOTH, None),
            P("expert", None, "dp"),
            P("expert", "dp", None),
            P(),
        ),
        out_specs=(P(BOTH, None), P()),
        check_vma=False,
    )
```

```python
import jax
import jax.numpy as jnp
from jax import lax
from jax.experimental import pallas as pl
from jax.experimental.pallas import tpu as pltpu
from jax.sharding import PartitionSpec as P

MESH = pl.DeviceIdType.MESH
BOTH = ("dp", "expert")
NX, NYH, NYL, NZ = 4, 2, 2, 8
NY = NYH * NYL
TILE = 16
GATES = 128
BF, F32 = jnp.bfloat16, jnp.float32


def coordinates():
    dp, ex = lax.axis_index("dp"), lax.axis_index("expert")
    x, yh = dp // NYH, dp % NYH
    core, zy = ex % 2, ex // 2
    return x, yh * NYL + zy % NYL, zy // NYL, core


class Part:
    def __init__(self, at, ring, quad, mid, refs, sems):
        self.at, self.ring, self.quad, self.mid = at, ring, quad, mid
        self.n, self.nq, self.m = ring[1], quad[1], mid[1]
        self.r = TILE * self.m
        self.T, self.ACC, self.SP, self.ST, self.S1, self.S4, self.SUM4, self.S5, self.SUM5, self.S6, self.OWN = refs
        self.sems = sems


def part_scratch(n, nq, m, width):
    r, q = TILE * m, width // nq
    shapes = [
        (2, n, r, width + GATES),
        (n, r, width),
        (2, r, width),
        (nq, TILE, q + GATES),
        (r, q + GATES),
        (nq, r, q),
        (r, q),
        (m, TILE, q),
        (TILE, q),
        (TILE, width),
        (r, width),
    ]
    counts = [(nq,), (m,), (m, nq), (n,), (n + 1,), (n + 1,), (m, nq), (m,), (nq,)]
    sems = [pltpu.SemaphoreType.DMA(c) for c in counts for _ in range(2)]
    sems += [pltpu.SemaphoreType.DMA((n + 1, 4)) for _ in range(2)]
    sems += [pltpu.SemaphoreType.REGULAR]
    return [pltpu.VMEM(s, BF) for s in shapes], sems


NBUF, NSEM = 11, 21


def kernel(x_ref, w1_hbm, w2_hbm, out_ref, mass_ref, *scratch):
    x, y, z, core = coordinates()
    sib_core = 1 - core
    d = 1 - 2 * core
    ex, dp = lax.axis_index("expert"), lax.axis_index("dp")
    width = out_ref.shape[2]
    half = w1_hbm.shape[2] // 2

    def dev(ax, i):
        if ax == "x":
            return (i * NYH + y // NYL, ex)
        if ax == "y":
            return (x * NYH + i // NYL, (z * NYL + i % NYL) * 2 + core)
        return (dp, (i * NYL + y % NYL) * 2 + core)

    sib = (dp, ex + d)
    axes = {"x": (x, NX, "x"), "y": (y, NY, "y"), "z": (z, NZ, "z")}
    specs = [("z", "y", "x"), ("x", "y", "z"), ("y", "x", "z")]
    parts = []
    for p, (a, b, c) in enumerate(specs):
        refs = scratch[p * NBUF : (p + 1) * NBUF]
        sems = scratch[3 * NBUF + p * NSEM : 3 * NBUF + (p + 1) * NSEM]
        parts.append(Part(p, axes[a], axes[b], axes[c], refs, sems))
    W1, W2, BOTHS, H, WSEM = scratch[3 * (NBUF + NSEM) :]

    loads = []
    for s in range(2):
        loads.append(
            pltpu.make_async_copy(
                w1_hbm.at[s], W1.at[:, pl.ds(s * 2 * half, 2 * half)], WSEM.at[s]
            )
        )
    loads.append(pltpu.make_async_copy(w2_hbm, W2, WSEM.at[2]))
    for load in loads:
        load.start()

    barrier = pltpu.get_barrier_semaphore()
    count = 1
    pl.semaphore_signal(barrier, inc=1, device_id=sib, device_id_type=MESH)
    for ax in "xyz":
        me, n, _ = axes[ax]
        for s in range(1, n):
            pl.semaphore_signal(
                barrier, inc=1, device_id=dev(ax, (me + s) % n), device_id_type=MESH
            )
            count += 1
    pl.semaphore_wait(barrier, count)

    def send(src, dst, ssem, rsem, to):
        pltpu.make_async_remote_copy(
            src_ref=src, dst_ref=dst, send_sem=ssem, recv_sem=rsem, device_id=to, device_id_type=MESH
        ).start()

    def got(dst, sem):
        pltpu.make_async_remote_copy(
            src_ref=dst, dst_ref=dst, send_sem=sem, recv_sem=sem, device_id=sib, device_id_type=MESH
        ).wait_recv()

    def sent(src, sem):
        pltpu.make_async_remote_copy(
            src_ref=src, dst_ref=src, send_sem=sem, recv_sem=sem, device_id=sib, device_id_type=MESH
        ).wait_send()

    def block(i, size):
        return pl.ds(pl.multiple_of(i * size, size), size)

    def own_chunk(p, t):
        return (p.ring[0] + p.n - d * t) % p.n

    def sib_chunk(p, t):
        return (p.ring[0] + p.n + d * t) % p.n

    def next_dev(p):
        return dev(p.ring[2], (p.ring[0] + p.n + d) % p.n)


    def nearest(n):
        return sorted(range(1, n), key=lambda s: min(s, n - s))

    def swap_quarters(p):
        me, n, ax = p.quad
        piece = p.ST.shape[2]
        for s in range(1, n):
            to = (me + s) % n
            send(x_ref.at[p.at, :, block(to, piece)], p.ST.at[me], p.sems[0].at[s], p.sems[1].at[s], dev(ax, to))

    def gather_rows(p):
        me, n, ax = p.quad
        piece = p.ST.shape[2]
        total = x_ref[p.at, :, block(me, piece)].astype(F32)
        for s in range(1, n):
            slot = (me + n - s) % n
            got(p.ST.at[slot], p.sems[1].at[s])
            total = total + p.ST[slot].astype(F32)
        mid, m, max_ = p.mid
        rows = block(mid, TILE)
        p.S1[rows, :] = total.astype(BF)
        for s in nearest(m):
            send(p.S1.at[rows], p.S1.at[rows], p.sems[2].at[s], p.sems[3].at[s], dev(max_, (mid + s) % m))

    def gather_quarters(p):
        mid, m, _ = p.mid
        me, n, ax = p.quad
        q = width // n
        mine = p.T.at[core, p.ring[0]]
        for s in [0] + nearest(m):
            rows = block((mid + m - s) % m, TILE)
            if s:
                got(p.S1.at[rows], p.sems[3].at[s])
            for u in range(1, n):
                send(p.S1.at[rows, pl.ds(0, q)], mine.at[rows, block(me, q)], p.sems[4].at[s, u], p.sems[5].at[s, u], dev(ax, (me + u) % n))
        p.T[core, p.ring[0], :, block(me, q)] = p.S1[:, :q]
        p.T[core, p.ring[0], :, width:] = p.S1[:, q:]

    def start_ring(p):
        mid, m, _ = p.mid
        me, n, ax = p.quad
        q = width // n
        for s in [0] + nearest(m):
            rows = block((mid + m - s) % m, TILE)
            for u in range(1, n):
                got(p.T.at[core, p.ring[0], rows, block((me + n - u) % n, q)], p.sems[5].at[s, u])
        chunk = p.T.at[core, p.ring[0]]
        send(chunk, chunk, p.sems[6].at[0], p.sems[7].at[0], next_dev(p))
        send(chunk, chunk, p.sems[8].at[p.n], p.sems[9].at[p.n], sib)

    A, B, C = parts
    for p in (A, C, B):
        swap_quarters(p)
    for p in (A, C, B):
        gather_rows(p)
    gather_quarters(A)
    start_ring(A)
    gather_quarters(C)
    gather_quarters(B)

    for load in loads:
        load.wait()

    tiles = 4
    tile = width // tiles
    lane = lax.broadcasted_iota(jnp.int32, (1, GATES), 1)
    experts_all = GATES // 2

    def forward(p, t):
        @pl.when(t < p.n)
        def _():
            chunk = p.T.at[core, own_chunk(p, t)]
            got(chunk, p.sems[7].at[t - 1])

            @pl.when(t < p.n - 1)
            def _():
                send(chunk, chunk, p.sems[6].at[t], p.sems[7].at[t], next_dev(p))

            send(chunk, chunk, p.sems[8].at[t], p.sems[9].at[t], sib)

    def compute(p, t):
        r = p.r
        jo, js = own_chunk(p, t), sib_chunk(p, t)
        got(p.T.at[sib_core, js], p.sems[9].at[t])
        rows = jnp.concatenate([p.T[core, jo, :, :width], p.T[sib_core, js, :, :width]], 0)
        BOTHS[: 2 * r] = jnp.dot(rows, W1[...], preferred_element_type=F32)
        gates = jnp.concatenate([p.T[core, jo, :, width:], p.T[sib_core, js, :, width:]], 0).astype(F32)
        g = []
        for s in range(2):
            e = 2 * ex + s
            pick = (lane == e) | (lane == e + experts_all)
            g.append(jnp.sum(jnp.where(pick, gates, 0.0), 1, keepdims=True))
        first, second = BOTHS[: 2 * r, : 2 * half], BOTHS[: 2 * r, 2 * half :]
        low = lax.broadcasted_iota(jnp.int32, (1, 2 * half), 1) < half
        gate = jnp.where(low, first, pltpu.roll(second, half, 1))
        up = jnp.where(low, pltpu.roll(first, half, 1), second)
        hidden = jax.nn.silu(gate) * up * jnp.where(low, g[0], g[1])
        H[: 2 * r] = hidden.astype(BF)

        def down(j, _):
            cols = block(j, tile)
            both = jnp.dot(H[: 2 * r], W2[:, cols], preferred_element_type=F32).astype(BF)
            p.OWN[:, cols] = both[:r]
            p.T[sib_core, js, :, cols] = both[r:]
            return 0

        lax.fori_loop(0, tiles, down, 0)

        @pl.when(t >= 3)
        def _():
            pl.semaphore_wait(p.sems[20], 1)

        send(p.T.at[sib_core, js, :, pl.ds(0, width)], p.SP.at[t % 2], p.sems[10].at[t], p.sems[11].at[t], sib)

    def combine(p, t):
        n, slot = p.n, t % 2
        got(p.SP.at[slot], p.sems[11].at[t])

        def add(j, _):
            cols = block(j, tile)
            here = p.ACC.at[t - 1, :, cols]

            @pl.when(t == 1)
            def _():
                here[...] = (p.OWN[:, cols].astype(F32) + p.SP[slot, :, cols].astype(F32)).astype(BF)

            @pl.when(t > 1)
            def _():
                got(here, p.sems[19].at[t - 1, j])
                total = p.OWN[:, cols].astype(F32) + p.SP[slot, :, cols].astype(F32)
                here[...] = (total + here[...].astype(F32)).astype(BF)

            @pl.when(t < n)
            def _():
                send(here, p.ACC.at[t, :, cols], p.sems[18].at[t, j], p.sems[19].at[t, j], next_dev(p))

            return 0

        lax.fori_loop(0, tiles, add, 0)

        @pl.when(t <= n - 2)
        def _():
            pl.semaphore_signal(p.sems[20], inc=1, device_id=sib, device_id_type=MESH)

    assert A.n == 2 * B.n and B.n == C.n

    def reduce_quarters(p):
        mid, m, _ = p.mid
        me, n, ax = p.quad
        q = width // n
        for s in nearest(m)[::-1] + [0]:
            rows = block((mid + s) % m, TILE)
            for u in range(1, n):
                to = (me + u) % n
                send(p.ACC.at[p.n - 1, rows, block(to, q)], p.S4.at[me, rows], p.sems[12].at[s, u], p.sems[13].at[s, u], dev(ax, to))

    def reduce_rows(p):
        mid, m, max_ = p.mid
        me, n, ax = p.quad
        q = width // n
        for s in nearest(m)[::-1] + [0]:
            to = (mid + s) % m
            rows = block(to, TILE)
            total = p.ACC[p.n - 1, rows, block(me, q)].astype(F32)
            for u in range(1, n):
                slot = (me + n - u) % n
                got(p.S4.at[slot, rows], p.sems[13].at[s, u])
                total = total + p.S4[slot, rows, :].astype(F32)
            p.SUM4[rows, :] = total.astype(BF)
            if s:
                send(p.SUM4.at[rows], p.S5.at[mid], p.sems[14].at[s], p.sems[15].at[s], dev(max_, to))

    def return_rows(p):
        mid, m, _ = p.mid
        total = p.SUM4[block(mid, TILE), :].astype(F32)
        for s in nearest(m)[::-1]:
            slot = (mid + m - s) % m
            got(p.S5.at[slot], p.sems[15].at[s])
            total = total + p.S5[slot].astype(F32)
        p.SUM5[...] = total.astype(BF)
        me, n, ax = p.quad
        q = width // n
        for s in range(1, n):
            send(p.SUM5, p.S6.at[:, block(me, q)], p.sems[16].at[s], p.sems[17].at[s], dev(ax, (me + s) % n))
        p.S6[:, block(me, q)] = p.SUM5[...]

    forward(A, 1)
    start_ring(C)
    start_ring(B)
    compute(A, 1)
    combine(A, 1)

    def last(k, f, p):
        @pl.when(k == B.n)
        def _():
            f(p)

    def odd(k, f):
        @pl.when(k < B.n)
        def _():
            f(A, 2 * k + 1)

    def round_(k, _):
        forward(A, 2 * k)
        compute(A, 2 * k)
        forward(B, k)
        forward(C, k)
        combine(A, 2 * k)
        last(k, reduce_quarters, A)
        compute(B, k)
        odd(k, forward)
        combine(B, k)
        last(k, reduce_quarters, B)
        odd(k, compute)
        compute(C, k)
        odd(k, combine)
        combine(C, k)
        last(k, reduce_quarters, C)
        return 0

    lax.fori_loop(1, B.n + 1, round_, 0)
    reduce_rows(A)
    reduce_rows(B)
    reduce_rows(C)
    return_rows(A)
    return_rows(B)
    return_rows(C)

    mass = jnp.zeros((TILE, GATES), F32)
    for p in parts:

        def add(i, m_, p=p):
            rows = p.T[i // p.n, i % p.n, :, width:].astype(F32)
            for j in range(p.m):
                m_ = m_ + rows[j * TILE : (j + 1) * TILE]
            return m_

        mass = lax.fori_loop(0, 2 * p.n, add, mass)
    mass_ref[...] = mass

    for p in parts:
        me, n, _ = p.quad
        q = width // n
        for s in range(1, n):
            got(p.S6.at[:, block((me + n - s) % n, q)], p.sems[17].at[s])
        out_ref[p.at] = p.S6[...]

    for p in parts:
        q = width // p.nq
        for s in range(1, p.nq):
            sent(p.ST.at[0], p.sems[0].at[s])
            sent(p.SUM5, p.sems[16].at[s])
            for g in range(p.m):
                sent(p.S1.at[pl.ds(0, TILE), pl.ds(0, q)], p.sems[4].at[g, s])
                sent(p.S4.at[0, pl.ds(0, TILE)], p.sems[12].at[g, s])
        for s in range(1, p.m):
            sent(p.S1.at[pl.ds(0, TILE)], p.sems[2].at[s])
            sent(p.S5.at[0], p.sems[14].at[s])

        def ring_sent(t, _, p=p):
            chunk = p.T.at[core, 0]

            @pl.when(t < p.n)
            def _():
                sent(chunk, p.sems[6].at[t - 1])
                for j in range(tiles):
                    sent(p.ACC.at[0, :, pl.ds(j * tile, tile)], p.sems[18].at[t, j])

            sent(chunk, p.sems[8].at[t])
            sent(p.SP.at[0], p.sems[10].at[t])
            return 0

        lax.fori_loop(1, p.n + 1, ring_sent, 0)


def fused(x, w1, w2, width):
    half = w1.shape[2] // 2
    buffers, sems = [], []
    for n, nq, m in ((NZ, NY, NX), (NX, NY, NZ), (NY, NX, NZ)):
        b, s = part_scratch(n, nq, m, width)
        buffers += b
        sems += s
    most = 2 * TILE * max(NX, NZ)
    return pl.pallas_call(
        kernel,
        out_shape=(
            jax.ShapeDtypeStruct((3, TILE, width), BF),
            jax.ShapeDtypeStruct((TILE, GATES), F32),
        ),
        in_specs=[
            pl.BlockSpec(memory_space=pltpu.VMEM),
            pl.BlockSpec(memory_space=pl.ANY),
            pl.BlockSpec(memory_space=pl.ANY),
        ],
        out_specs=(pl.BlockSpec(memory_space=pltpu.VMEM), pl.BlockSpec(memory_space=pltpu.VMEM)),
        scratch_shapes=[
            *buffers,
            *sems,
            pltpu.VMEM((width, 4 * half), BF),
            pltpu.VMEM((2 * half, width), BF),
            pltpu.VMEM((most, 4 * half), F32),
            pltpu.VMEM((most, 2 * half), BF),
            pltpu.SemaphoreType.DMA((3,)),
        ],
        compiler_params=pltpu.CompilerParams(
            collective_id=0, has_side_effects=True, vmem_limit_bytes=VMEM_LIMIT
        ),
        cost_estimate=pl.CostEstimate(flops=30_000_000_000, bytes_accessed=10_000_000, transcendentals=1_200_000),
    )(x, w1, w2)


VMEM_LIMIT = 63 * 2**20


def planned_load(mass, swap_slot, per_device, owners, tokens_all):
    experts = jnp.arange(mass.shape[0], dtype=jnp.int32)
    home, within = experts // per_device, experts % per_device
    slot = jnp.repeat(swap_slot, per_device)
    holder = jnp.where(within == slot, (home + owners // 2) % owners, home)
    hot = holder[:, None] == jnp.arange(owners, dtype=jnp.int32)
    return jnp.sum(jnp.where(hot, mass[:, None], 0.0), 0) * (owners / tokens_all)


def on_device(tokens, expert_ids, gate_probs, in_weight, out_weight, swap_slot):
    owners, groups = lax.axis_size("expert"), lax.axis_size("dp")
    per_device, width = in_weight.shape[:2]
    half = out_weight.shape[1]
    experts_all = GATES // 2
    experts = jnp.arange(experts_all, dtype=jnp.int32)
    dense = jnp.sum(
        jnp.where(expert_ids[..., None] == experts, gate_probs[..., None], 0.0), 1
    )
    high = lax.reduce_precision(dense, 8, 7)
    gates = jnp.concatenate([high, dense - high], 1).astype(BF)
    x, y, _, _ = coordinates()
    rows = tokens.shape[0] // 3
    blocks = []
    for p, (at, lines) in enumerate(((y, NY), (y, NY), (x, NX))):
        q = width // lines
        mine = slice(p * rows, (p + 1) * rows)
        wide = jnp.concatenate(
            [tokens[mine].reshape(rows, lines, q), jnp.broadcast_to(gates[mine, None], (rows, lines, GATES))], 2
        ).reshape(rows, -1)
        zero = jnp.zeros((TILE, wide.shape[1]), BF)
        blocks.append(lax.dynamic_update_slice_in_dim(zero, wide, at * rows, 0))
    mixed, mass = fused(jnp.stack(blocks), in_weight, out_weight.reshape(per_device * half, width), width)
    out = jnp.concatenate(
        [lax.dynamic_slice_in_dim(mixed[p], at * rows, rows, 0) for p, at in enumerate((y, y, x))], 0
    )
    mass = jnp.sum(mass, 0)
    mass = (mass[:experts_all] + mass[experts_all:])[: per_device * owners]
    load = planned_load(mass, swap_slot, per_device, owners, groups * owners * tokens.shape[0])
    return out, load


def solution(mesh):
    return jax.shard_map(
        on_device,
        mesh=mesh,
        in_specs=(
            P(BOTH, None),
            P(BOTH, None),
            P(BOTH, None),
            P("expert", None, "dp"),
            P("expert", "dp", None),
            P(),
        ),
        out_specs=(P(BOTH, None), P()),
        check_vma=False,
    )
```

```python
import jax
import jax.numpy as jnp
from jax import lax
from jax.experimental import pallas as pl
from jax.experimental.pallas import tpu as pltpu
from jax.sharding import PartitionSpec as P

MESH = pl.DeviceIdType.MESH
BOTH = ("dp", "expert")
NX, NYH, NYL, NZ = 4, 2, 2, 8
NY = NYH * NYL
TILE = 16
GATES = 128
BF, F32 = jnp.bfloat16, jnp.float32


def coordinates():
    dp, ex = lax.axis_index("dp"), lax.axis_index("expert")
    x, yh = dp // NYH, dp % NYH
    core, zy = ex % 2, ex // 2
    return x, yh * NYL + zy % NYL, zy // NYL, core


class Part:
    def __init__(self, at, ring, quad, mid, refs, sems):
        self.at, self.ring, self.quad, self.mid = at, ring, quad, mid
        self.n, self.nq, self.m = ring[1], quad[1], mid[1]
        self.r = TILE * self.m
        self.T, self.ACC, self.SP, self.ST, self.S1, self.S4, self.SUM4, self.S5, self.SUM5, self.S6, self.OWN = refs
        self.sems = sems


def part_scratch(n, nq, m, width):
    r, q = TILE * m, width // nq
    shapes = [
        (2, n, r, width + GATES),
        (n, r, width),
        (2, r, width),
        (nq, TILE, q + GATES),
        (r, q + GATES),
        (nq, r, q),
        (r, q),
        (m, TILE, q),
        (TILE, q),
        (TILE, width),
        (r, width),
    ]
    counts = [(nq,), (m,), (m, nq), (n,), (n + 1,), (n + 1,), (m, nq), (m,), (nq,)]
    sems = [pltpu.SemaphoreType.DMA(c) for c in counts for _ in range(2)]
    sems += [pltpu.SemaphoreType.DMA((n + 1, 4)) for _ in range(2)]
    sems += [pltpu.SemaphoreType.REGULAR]
    return [pltpu.VMEM(s, BF) for s in shapes], sems


NBUF, NSEM = 11, 21


def kernel(x_ref, w1_hbm, w2_hbm, out_ref, mass_ref, *scratch):
    x, y, z, core = coordinates()
    sib_core = 1 - core
    d = 1 - 2 * core
    ex, dp = lax.axis_index("expert"), lax.axis_index("dp")
    width = out_ref.shape[2]
    half = w1_hbm.shape[2] // 2

    def dev(ax, i):
        if ax == "x":
            return (i * NYH + y // NYL, ex)
        if ax == "y":
            return (x * NYH + i // NYL, (z * NYL + i % NYL) * 2 + core)
        return (dp, (i * NYL + y % NYL) * 2 + core)

    sib = (dp, ex + d)
    axes = {"x": (x, NX, "x"), "y": (y, NY, "y"), "z": (z, NZ, "z")}
    specs = [("z", "y", "x"), ("x", "y", "z"), ("y", "x", "z")]
    parts = []
    for p, (a, b, c) in enumerate(specs):
        refs = scratch[p * NBUF : (p + 1) * NBUF]
        sems = scratch[3 * NBUF + p * NSEM : 3 * NBUF + (p + 1) * NSEM]
        parts.append(Part(p, axes[a], axes[b], axes[c], refs, sems))
    W1, W2, BOTHS, H, WSEM = scratch[3 * (NBUF + NSEM) :]

    loads = []
    for s in range(2):
        loads.append(
            pltpu.make_async_copy(
                w1_hbm.at[s], W1.at[:, pl.ds(s * 2 * half, 2 * half)], WSEM.at[s]
            )
        )
    loads.append(pltpu.make_async_copy(w2_hbm, W2, WSEM.at[2]))
    for load in loads:
        load.start()

    barrier = pltpu.get_barrier_semaphore()
    count = 1
    pl.semaphore_signal(barrier, inc=1, device_id=sib, device_id_type=MESH)
    for ax in "xyz":
        me, n, _ = axes[ax]
        for s in range(1, n):
            pl.semaphore_signal(
                barrier, inc=1, device_id=dev(ax, (me + s) % n), device_id_type=MESH
            )
            count += 1
    pl.semaphore_wait(barrier, count)

    def send(src, dst, ssem, rsem, to):
        pltpu.make_async_remote_copy(
            src_ref=src, dst_ref=dst, send_sem=ssem, recv_sem=rsem, device_id=to, device_id_type=MESH
        ).start()

    def got(dst, sem):
        pltpu.make_async_remote_copy(
            src_ref=dst, dst_ref=dst, send_sem=sem, recv_sem=sem, device_id=sib, device_id_type=MESH
        ).wait_recv()

    def sent(src, sem):
        pltpu.make_async_remote_copy(
            src_ref=src, dst_ref=src, send_sem=sem, recv_sem=sem, device_id=sib, device_id_type=MESH
        ).wait_send()

    def block(i, size):
        return pl.ds(pl.multiple_of(i * size, size), size)

    def own_chunk(p, t):
        return (p.ring[0] + p.n - d * t) % p.n

    def sib_chunk(p, t):
        return (p.ring[0] + p.n + d * t) % p.n

    def next_dev(p):
        return dev(p.ring[2], (p.ring[0] + p.n + d) % p.n)


    def nearest(n):
        return sorted(range(1, n), key=lambda s: min(s, n - s))

    def swap_quarters(p):
        me, n, ax = p.quad
        piece = p.ST.shape[2]
        for s in range(1, n):
            to = (me + s) % n
            send(x_ref.at[p.at, :, block(to, piece)], p.ST.at[me], p.sems[0].at[s], p.sems[1].at[s], dev(ax, to))

    def gather_rows(p):
        me, n, ax = p.quad
        piece = p.ST.shape[2]
        total = x_ref[p.at, :, block(me, piece)].astype(F32)
        for s in range(1, n):
            slot = (me + n - s) % n
            got(p.ST.at[slot], p.sems[1].at[s])
            total = total + p.ST[slot].astype(F32)
        mid, m, max_ = p.mid
        rows = block(mid, TILE)
        p.S1[rows, :] = total.astype(BF)
        for s in nearest(m):
            send(p.S1.at[rows], p.S1.at[rows], p.sems[2].at[s], p.sems[3].at[s], dev(max_, (mid + s) % m))

    def gather_quarters(p):
        mid, m, _ = p.mid
        me, n, ax = p.quad
        q = width // n
        mine = p.T.at[core, p.ring[0]]
        for s in [0] + nearest(m):
            rows = block((mid + m - s) % m, TILE)
            if s:
                got(p.S1.at[rows], p.sems[3].at[s])
            for u in range(1, n):
                send(p.S1.at[rows, pl.ds(0, q)], mine.at[rows, block(me, q)], p.sems[4].at[s, u], p.sems[5].at[s, u], dev(ax, (me + u) % n))
        p.T[core, p.ring[0], :, block(me, q)] = p.S1[:, :q]
        p.T[core, p.ring[0], :, width:] = p.S1[:, q:]

    def start_ring(p):
        mid, m, _ = p.mid
        me, n, ax = p.quad
        q = width // n
        for s in [0] + nearest(m):
            rows = block((mid + m - s) % m, TILE)
            for u in range(1, n):
                got(p.T.at[core, p.ring[0], rows, block((me + n - u) % n, q)], p.sems[5].at[s, u])
        chunk = p.T.at[core, p.ring[0]]
        send(chunk, chunk, p.sems[6].at[0], p.sems[7].at[0], next_dev(p))
        send(chunk, chunk, p.sems[8].at[p.n], p.sems[9].at[p.n], sib)

    A, B, C = parts
    for p in (A, C, B):
        swap_quarters(p)
    for p in (A, C, B):
        gather_rows(p)
    gather_quarters(A)
    start_ring(A)
    gather_quarters(C)
    gather_quarters(B)

    for load in loads:
        load.wait()

    tiles = 4
    tile = width // tiles
    lane = lax.broadcasted_iota(jnp.int32, (1, GATES), 1)
    experts_all = GATES // 2

    def forward(p, t):
        @pl.when(t < p.n)
        def _():
            chunk = p.T.at[core, own_chunk(p, t)]
            got(chunk, p.sems[7].at[t - 1])

            @pl.when(t < p.n - 1)
            def _():
                send(chunk, chunk, p.sems[6].at[t], p.sems[7].at[t], next_dev(p))

            send(chunk, chunk, p.sems[8].at[t], p.sems[9].at[t], sib)

    def compute(p, t):
        r = p.r
        jo, js = own_chunk(p, t), sib_chunk(p, t)
        got(p.T.at[sib_core, js], p.sems[9].at[t])
        rows = jnp.concatenate([p.T[core, jo, :, :width], p.T[sib_core, js, :, :width]], 0)
        BOTHS[: 2 * r] = jnp.dot(rows, W1[...], preferred_element_type=F32)
        gates = jnp.concatenate([p.T[core, jo, :, width:], p.T[sib_core, js, :, width:]], 0).astype(F32)
        g = []
        for s in range(2):
            e = 2 * ex + s
            pick = (lane == e) | (lane == e + experts_all)
            g.append(jnp.sum(jnp.where(pick, gates, 0.0), 1, keepdims=True))
        first, second = BOTHS[: 2 * r, : 2 * half], BOTHS[: 2 * r, 2 * half :]
        low = lax.broadcasted_iota(jnp.int32, (1, 2 * half), 1) < half
        gate = jnp.where(low, first, pltpu.roll(second, half, 1))
        up = jnp.where(low, pltpu.roll(first, half, 1), second)
        hidden = jax.nn.silu(gate) * up * jnp.where(low, g[0], g[1])
        H[: 2 * r] = hidden.astype(BF)

        def down(j, _):
            cols = block(j, tile)
            both = jnp.dot(H[: 2 * r], W2[:, cols], preferred_element_type=F32).astype(BF)
            p.OWN[:, cols] = both[:r]
            p.T[sib_core, js, :, cols] = both[r:]
            return 0

        lax.fori_loop(0, tiles, down, 0)

        @pl.when(t >= 3)
        def _():
            pl.semaphore_wait(p.sems[20], 1)

        send(p.T.at[sib_core, js, :, pl.ds(0, width)], p.SP.at[t % 2], p.sems[10].at[t], p.sems[11].at[t], sib)

    def combine(p, t):
        n, slot = p.n, t % 2
        got(p.SP.at[slot], p.sems[11].at[t])

        def add(j, _):
            cols = block(j, tile)
            here = p.ACC.at[t - 1, :, cols]

            @pl.when(t == 1)
            def _():
                here[...] = (p.OWN[:, cols].astype(F32) + p.SP[slot, :, cols].astype(F32)).astype(BF)

            @pl.when(t > 1)
            def _():
                got(here, p.sems[19].at[t - 1, j])
                total = p.OWN[:, cols].astype(F32) + p.SP[slot, :, cols].astype(F32)
                here[...] = (total + here[...].astype(F32)).astype(BF)

            @pl.when(t < n)
            def _():
                send(here, p.ACC.at[t, :, cols], p.sems[18].at[t, j], p.sems[19].at[t, j], next_dev(p))

            return 0

        lax.fori_loop(0, tiles, add, 0)

        @pl.when(t <= n - 2)
        def _():
            pl.semaphore_signal(p.sems[20], inc=1, device_id=sib, device_id_type=MESH)

    assert A.n == 2 * B.n and B.n == C.n

    def reduce_quarters(p):
        mid, m, _ = p.mid
        me, n, ax = p.quad
        q = width // n
        for s in nearest(m)[::-1] + [0]:
            rows = block((mid + s) % m, TILE)
            for u in range(1, n):
                to = (me + u) % n
                send(p.ACC.at[p.n - 1, rows, block(to, q)], p.S4.at[me, rows], p.sems[12].at[s, u], p.sems[13].at[s, u], dev(ax, to))

    def reduce_rows(p):
        mid, m, max_ = p.mid
        me, n, ax = p.quad
        q = width // n
        for s in nearest(m)[::-1] + [0]:
            to = (mid + s) % m
            rows = block(to, TILE)
            total = p.ACC[p.n - 1, rows, block(me, q)].astype(F32)
            for u in range(1, n):
                slot = (me + n - u) % n
                got(p.S4.at[slot, rows], p.sems[13].at[s, u])
                total = total + p.S4[slot, rows, :].astype(F32)
            p.SUM4[rows, :] = total.astype(BF)
            if s:
                send(p.SUM4.at[rows], p.S5.at[mid], p.sems[14].at[s], p.sems[15].at[s], dev(max_, to))

    def return_rows(p):
        mid, m, _ = p.mid
        total = p.SUM4[block(mid, TILE), :].astype(F32)
        for s in nearest(m)[::-1]:
            slot = (mid + m - s) % m
            got(p.S5.at[slot], p.sems[15].at[s])
            total = total + p.S5[slot].astype(F32)
        p.SUM5[...] = total.astype(BF)
        me, n, ax = p.quad
        q = width // n
        for s in range(1, n):
            send(p.SUM5, p.S6.at[:, block(me, q)], p.sems[16].at[s], p.sems[17].at[s], dev(ax, (me + s) % n))
        p.S6[:, block(me, q)] = p.SUM5[...]

    forward(A, 1)
    start_ring(C)
    start_ring(B)
    compute(A, 1)
    combine(A, 1)

    def last(k, f, p):
        @pl.when(k == B.n)
        def _():
            f(p)

    def odd(k, f):
        @pl.when(k < B.n)
        def _():
            f(A, 2 * k + 1)

    def round_(k, _):
        forward(A, 2 * k)
        compute(A, 2 * k)
        forward(C, k)
        forward(B, k)
        combine(A, 2 * k)
        last(k, reduce_quarters, A)
        compute(C, k)
        odd(k, forward)
        compute(B, k)
        combine(C, k)
        last(k, reduce_quarters, C)
        odd(k, compute)
        odd(k, combine)
        last(k, reduce_rows, A)
        combine(B, k)
        last(k, reduce_quarters, B)
        return 0

    lax.fori_loop(1, B.n + 1, round_, 0)
    reduce_rows(C)
    reduce_rows(B)
    return_rows(A)
    return_rows(B)
    return_rows(C)

    mass = jnp.zeros((TILE, GATES), F32)
    for p in parts:

        def add(i, m_, p=p):
            rows = p.T[i // p.n, i % p.n, :, width:].astype(F32)
            for j in range(p.m):
                m_ = m_ + rows[j * TILE : (j + 1) * TILE]
            return m_

        mass = lax.fori_loop(0, 2 * p.n, add, mass)
    mass_ref[...] = mass

    for p in parts:
        me, n, _ = p.quad
        q = width // n
        for s in range(1, n):
            got(p.S6.at[:, block((me + n - s) % n, q)], p.sems[17].at[s])
        out_ref[p.at] = p.S6[...]

    for p in parts:
        q = width // p.nq
        for s in range(1, p.nq):
            sent(p.ST.at[0], p.sems[0].at[s])
            sent(p.SUM5, p.sems[16].at[s])
            for g in range(p.m):
                sent(p.S1.at[pl.ds(0, TILE), pl.ds(0, q)], p.sems[4].at[g, s])
                sent(p.S4.at[0, pl.ds(0, TILE)], p.sems[12].at[g, s])
        for s in range(1, p.m):
            sent(p.S1.at[pl.ds(0, TILE)], p.sems[2].at[s])
            sent(p.S5.at[0], p.sems[14].at[s])

        def ring_sent(t, _, p=p):
            chunk = p.T.at[core, 0]

            @pl.when(t < p.n)
            def _():
                sent(chunk, p.sems[6].at[t - 1])
                for j in range(tiles):
                    sent(p.ACC.at[0, :, pl.ds(j * tile, tile)], p.sems[18].at[t, j])

            sent(chunk, p.sems[8].at[t])
            sent(p.SP.at[0], p.sems[10].at[t])
            return 0

        lax.fori_loop(1, p.n + 1, ring_sent, 0)


def fused(x, w1, w2, width):
    half = w1.shape[2] // 2
    buffers, sems = [], []
    for n, nq, m in ((NZ, NY, NX), (NX, NY, NZ), (NY, NX, NZ)):
        b, s = part_scratch(n, nq, m, width)
        buffers += b
        sems += s
    most = 2 * TILE * max(NX, NZ)
    return pl.pallas_call(
        kernel,
        out_shape=(
            jax.ShapeDtypeStruct((3, TILE, width), BF),
            jax.ShapeDtypeStruct((TILE, GATES), F32),
        ),
        in_specs=[
            pl.BlockSpec(memory_space=pltpu.VMEM),
            pl.BlockSpec(memory_space=pl.ANY),
            pl.BlockSpec(memory_space=pl.ANY),
        ],
        out_specs=(pl.BlockSpec(memory_space=pltpu.VMEM), pl.BlockSpec(memory_space=pltpu.VMEM)),
        scratch_shapes=[
            *buffers,
            *sems,
            pltpu.VMEM((width, 4 * half), BF),
            pltpu.VMEM((2 * half, width), BF),
            pltpu.VMEM((most, 4 * half), F32),
            pltpu.VMEM((most, 2 * half), BF),
            pltpu.SemaphoreType.DMA((3,)),
        ],
        compiler_params=pltpu.CompilerParams(
            collective_id=0, has_side_effects=True, vmem_limit_bytes=VMEM_LIMIT
        ),
        cost_estimate=pl.CostEstimate(flops=30_000_000_000, bytes_accessed=10_000_000, transcendentals=1_200_000),
    )(x, w1, w2)


VMEM_LIMIT = 63 * 2**20


def planned_load(mass, swap_slot, per_device, owners, tokens_all):
    experts = jnp.arange(mass.shape[0], dtype=jnp.int32)
    home, within = experts // per_device, experts % per_device
    slot = jnp.repeat(swap_slot, per_device)
    holder = jnp.where(within == slot, (home + owners // 2) % owners, home)
    hot = holder[:, None] == jnp.arange(owners, dtype=jnp.int32)
    return jnp.sum(jnp.where(hot, mass[:, None], 0.0), 0) * (owners / tokens_all)


def on_device(tokens, expert_ids, gate_probs, in_weight, out_weight, swap_slot):
    owners, groups = lax.axis_size("expert"), lax.axis_size("dp")
    per_device, width = in_weight.shape[:2]
    half = out_weight.shape[1]
    experts_all = GATES // 2
    experts = jnp.arange(experts_all, dtype=jnp.int32)
    dense = jnp.sum(
        jnp.where(expert_ids[..., None] == experts, gate_probs[..., None], 0.0), 1
    )
    high = lax.reduce_precision(dense, 8, 7)
    gates = jnp.concatenate([high, dense - high], 1).astype(BF)
    x, y, _, _ = coordinates()
    rows = tokens.shape[0] // 3
    blocks = []
    for p, (at, lines) in enumerate(((y, NY), (y, NY), (x, NX))):
        q = width // lines
        mine = slice(p * rows, (p + 1) * rows)
        wide = jnp.concatenate(
            [tokens[mine].reshape(rows, lines, q), jnp.broadcast_to(gates[mine, None], (rows, lines, GATES))], 2
        ).reshape(rows, -1)
        zero = jnp.zeros((TILE, wide.shape[1]), BF)
        blocks.append(lax.dynamic_update_slice_in_dim(zero, wide, at * rows, 0))
    mixed, mass = fused(jnp.stack(blocks), in_weight, out_weight.reshape(per_device * half, width), width)
    out = jnp.concatenate(
        [lax.dynamic_slice_in_dim(mixed[p], at * rows, rows, 0) for p, at in enumerate((y, y, x))], 0
    )
    mass = jnp.sum(mass, 0)
    mass = (mass[:experts_all] + mass[experts_all:])[: per_device * owners]
    load = planned_load(mass, swap_slot, per_device, owners, groups * owners * tokens.shape[0])
    return out, load


def solution(mesh):
    return jax.shard_map(
        on_device,
        mesh=mesh,
        in_specs=(
            P(BOTH, None),
            P(BOTH, None),
            P(BOTH, None),
            P("expert", None, "dp"),
            P("expert", "dp", None),
            P(),
        ),
        out_specs=(P(BOTH, None), P()),
        check_vma=False,
    )
```
